32 devices in a mesh: replica: 16 (over z, x, core), shard: 2 (over y).
Axes of the slice: x: 2, y: 2, z: 4, core: 2. Of those that a mesh axis runs over, the one named last changes fastest.
Arguments:
- tokens: bfloat16 [16, 512, 4096], P('replica', 'shard'), may hold values from -6 to 6
- key_grads: bfloat16 [16, 512, 512], P('replica', 'shard'), may hold values from -6 to 6
- numerator: float32 [16, 4096, 512], P('replica', 'shard'), may hold values from -0.09375 to 0.09375
- push_weight: float32 [16], P('replica'), may hold values from 0.5 to 2
- train_step: int32 [], replicated, may hold values from 0 to 999
Outputs:
- keys_after: bfloat16 [16, 512, 512], P('replica', 'shard')
- mixed_numerator: float32 [16, 4096, 512], P('replica', 'shard')
- mixed_weight: float32 [16], P('replica')
The draws below stay inside these ranges and needn't reach their ends.
All inputs are finite; a program needn't handle non-finite values.
Results may differ from the reference program's by a relative error of at most 0.0085.
Values may be sent and summed in bfloat16 or wider, within the bound.
No kernel may reach another device: no remote copies, remote signals or barrier semaphores. Data moves between devices by JAX's collectives and lax.ppermute only.
A program may use at most 64 MiB of HBM per device.

```python
import math
import jax
import jax.numpy as jnp
from jax import lax

D_IN = 4096
TOK_DEV = 256
KC = 512
SHARDS = 2
REP_TOK = 512
REPLICAS = 16


def steps_of(stream_key, dims, split, low, high):
    def one(dim, blocks):
        heights = jax.random.uniform(jax.random.fold_in(jax.random.fold_in(stream_key, 6), dim), (blocks,), jnp.float32, low / len(split), high / len(split))
        return jnp.repeat(jnp.exp(heights), dims[dim] // blocks).reshape((-1,) + (1,) * (len(dims) - dim - 1))

    gain = one(*split[0])
    for cut in split[1:]:
        gain = gain * one(*cut)
    return gain


def gaussian(own_key, extent, scale, limit, cuts=(), held_as=jnp.bfloat16):
    drawn = scale * jax.random.normal(own_key, extent, jnp.float32)
    if cuts:
        drawn = drawn * steps_of(own_key, extent, cuts, -0.22, 0.18)
    return jnp.clip(drawn, -limit, limit).astype(held_as)


def setup_inputs(seed: int = 0) -> dict:
    keys = jax.random.split(jax.random.key(seed), 6)
    return {
        "tokens": gaussian(keys[0], (REPLICAS, REP_TOK, D_IN), 1.0, 6.0, ((0, 16), (1, 2))),
        "key_grads": gaussian(keys[1], (REPLICAS, REP_TOK, KC), 1.0, 6.0, ((0, 16), (1, 2))),
        "numerator": gaussian(keys[2], (REPLICAS, D_IN, KC), D_IN ** -0.5, 0.09375, ((0, 16), (1, 2)), jnp.float32),
        "push_weight": jnp.clip(jnp.exp(math.log(2.0) - 1.3862944 * jax.random.uniform(keys[3], (REPLICAS,), jnp.float32) ** steps_of(keys[3], (REPLICAS,), ((0, 16),), -0.2, 0.2)), 0.5, 2.0),
        "train_step": jax.random.randint(keys[4], (), 0, 1000).astype(jnp.int32),
    }


learn_rate = 0.5


def gradient_one(operands):
    features, upstream = operands
    blocks_x = features.reshape(SHARDS, TOK_DEV, D_IN).astype(jnp.float32)
    blocks_g = upstream.reshape(SHARDS, TOK_DEV, KC).astype(jnp.float32)
    partial_value = jnp.einsum("ntr,ntk->nrk", blocks_x, blocks_g).astype(jnp.bfloat16)
    partial_value = lax.optimization_barrier(partial_value)
    return jnp.sum(partial_value.astype(jnp.float32), axis=0) / jnp.float32(REP_TOK)


def keys_one(operands):
    features, weights = operands
    return jnp.dot(features, weights, preferred_element_type=jnp.float32).astype(jnp.bfloat16)


def reference(tokens, key_grads, numerator, push_weight, train_step):
    offset = (jnp.left_shift(jnp.int32(1), jnp.remainder(train_step, 5).astype(jnp.int32)) % REPLICAS).astype(jnp.int32)
    gradient = lax.map(gradient_one, (tokens, key_grads))
    updated = numerator - learn_rate * gradient
    mixed_numerator = 0.5 * updated + 0.5 * jnp.roll(updated, offset, axis=0)
    mixed_weight = 0.5 * push_weight + 0.5 * jnp.roll(push_weight, offset, axis=0)
    debiased = (mixed_numerator / mixed_weight[:, None, None]).astype(jnp.bfloat16)
    keys_after = lax.map(keys_one, (tokens, debiased))
    return (keys_after, mixed_numerator, mixed_weight)
```

```python
from functools import partial

import jax
import jax.numpy as jnp
from jax import lax
from jax.experimental import pallas as pl
from jax.experimental.pallas import tpu as pltpu
from jax.sharding import PartitionSpec as P

learn_rate = 0.5
params = pltpu.CompilerParams(vmem_limit_bytes=48 * 1024 * 1024)


def shifted(value, axis, by):
    count = lax.axis_size(axis)
    return lax.ppermute(value, axis, [(i, (i + by) % count) for i in range(count)])


def cuts(rows, distance):
    if rows != 2048:
        return [(0, rows // 2), (rows // 2, rows // 2)]
    if distance == 0:
        sizes = [1024, 1024]
    elif distance == 1:
        sizes = [512, 1024, 512]
    else:
        sizes = [256, 512, 1024, 256]
    out, at = [], 0
    for size in sizes:
        out.append((at, size))
        at += size
    return out


def cost(flops, size):
    return pl.CostEstimate(flops=flops, bytes_accessed=size, transcendentals=0)


def half_updated(total, tok, key_grads, other_tok, other_grads, numerator):
    toks = key_grads.shape[0]
    dims = (((0,), (0,)), ((), ()))
    summed = lax.dot_general(tok, key_grads, dims, preferred_element_type=jnp.float32)
    summed = summed.astype(jnp.bfloat16).astype(jnp.float32)
    for j in range(other_grads.shape[0] // toks):
        own = slice(j * toks, (j + 1) * toks)
        part = lax.dot_general(other_tok[own], other_grads[own], dims, preferred_element_type=jnp.float32)
        summed += part.astype(jnp.bfloat16).astype(jnp.float32)
    updated = numerator - learn_rate * (summed / jnp.float32(total))
    return 0.5 * updated


def update_kernel(total, shard, tok, key_grads, other_tok, other_grads, numerator, half, sent):
    value = half_updated(total, tok[...], key_grads[...], other_tok[...], other_grads[...], numerator[0])
    half[...] = value
    sent[...] = value.astype(jnp.bfloat16)


def keys_step(tok, other_tok, debiased, sums, other_sums, before):
    step = pl.program_id(0)
    own = jnp.dot(tok[...], debiased, preferred_element_type=jnp.float32)
    other = jnp.dot(other_tok[...], debiased, preferred_element_type=jnp.float32)

    @pl.when(step == 0)
    def _():
        if before is None:
            sums[...] = own
            other_sums[...] = other
        else:
            sums[...] = before[0][...] + own
            other_sums[...] = before[1][...] + other

    @pl.when(step > 0)
    def _():
        sums[...] += own
        other_sums[...] += other


def mix_kernel(first, shard, weight, half, received, tok, other_tok, *rest):
    mixed_in, before = (None, None) if first else (rest[0], rest[1:3])
    mixed, sums, other_sums = rest[-3:]
    value = half[...] + received[...].astype(jnp.float32)
    mixed[0] = value
    debiased = (value / weight[0]).astype(jnp.bfloat16)
    keys_step(tok, other_tok, debiased, sums, other_sums, before)


def local_kernel(total, first, shard, weight, tok, key_grads, other_tok, other_grads, numerator, *rest):
    mixed_in, before = (None, None) if first else (rest[0], rest[1:3])
    mixed, sums, other_sums = rest[-3:]
    value = half_updated(total, tok[...], key_grads[...], other_tok[...], other_grads[...], numerator[0])
    value = value + value
    mixed[0] = value
    debiased = (value / weight[0]).astype(jnp.bfloat16)
    keys_step(tok, other_tok, debiased, sums, other_sums, before)


def branch(tokens, key_grads, numerator, push_weight, distance):
    shards = lax.axis_size("shard")
    shard = lax.axis_index("shard")
    index = shard.astype(jnp.int32)[None]
    tok, grads = tokens[0], key_grads[0]
    toks, cols = grads.shape
    rows = numerator.shape[1]
    total = toks * shards
    others = (shards - 1) * toks
    size = min(256, rows // 2)
    pieces = cuts(rows, distance)

    messages = []
    for c, (at, length) in enumerate(pieces):
        arrived = []
        for step in range(1, shards):
            peer = lax.rem(shard + step, shards)
            part = lax.dynamic_slice_in_dim(tok, peer * rows + at, length, axis=1)
            if c == 0:
                part = jnp.concatenate([grads, part], axis=1)
            arrived.append(shifted(part, "shard", step))
        messages.append(arrived[0] if shards == 2 else jnp.concatenate(arrived, axis=0))
    leads = [cols if c == 0 else 0 for c in range(len(pieces))]

    half_weight = 0.5 * push_weight
    mixed_weight = half_weight + (half_weight if distance == 0 else shifted(half_weight, "replica", distance))

    def spec_tok(at):
        return pl.BlockSpec((toks, size), lambda i, s: (0, s[0] * (rows // size) + at // size + i))

    def spec_other(lead):
        return pl.BlockSpec((others, size), lambda i, s: (0, lead // size + i))

    def spec_rows(at):
        return pl.BlockSpec((1, size, cols), lambda i, s: (0, at // size + i, 0))

    spec_grads = pl.BlockSpec((toks, cols), lambda i, s: (0, 0))
    spec_other_grads = pl.BlockSpec((others, cols), lambda i, s: (0, 0))
    spec_chunk = pl.BlockSpec((size, cols), lambda i, s: (i, 0))
    spec_weight = pl.BlockSpec(memory_space=pltpu.SMEM)
    spec_mixed = pl.BlockSpec(memory_space=pl.ANY)
    shape_mixed = jax.ShapeDtypeStruct(numerator.shape, jnp.float32)
    shape_sums = [jax.ShapeDtypeStruct((toks, cols), jnp.float32), jax.ShapeDtypeStruct((others, cols), jnp.float32)]

    def call(kernel, length, ins, specs, out_specs, out_shapes, aliases, flops):
        grid_spec = pltpu.PrefetchScalarGridSpec(
            num_scalar_prefetch=1, grid=(length // size,), in_specs=specs, out_specs=out_specs
        )
        return pl.pallas_call(
            kernel,
            grid_spec=grid_spec,
            out_shape=out_shapes,
            input_output_aliases=aliases,
            compiler_params=params,
            cost_estimate=cost(flops, length * cols * 10),
        )(index, *ins)

    flops = [2 * length * total * cols for _, length in pieces]
    carried = []
    if distance == 0:
        for c, (at, length) in enumerate(pieces):
            ins = [mixed_weight, tok, grads, messages[c], messages[0], numerator] + carried
            specs = [spec_weight, spec_tok(at), spec_grads, spec_other(leads[c]), spec_other_grads, spec_rows(at)]
            if carried:
                specs += [spec_mixed, spec_grads, spec_other_grads]
            carried = list(call(
                partial(local_kernel, total, c == 0), length, ins, specs,
                [spec_rows(at), spec_grads, spec_other_grads], [shape_mixed] + shape_sums,
                {7: 0} if carried else {}, 2 * flops[c],
            ))
    else:
        halves, received = [], []
        for c, (at, length) in enumerate(pieces):
            half, sent = call(
                partial(update_kernel, total), length,
                [tok, grads, messages[c], messages[0], numerator],
                [spec_tok(at), spec_grads, spec_other(leads[c]), spec_other_grads, spec_rows(at)],
                [spec_chunk, spec_chunk],
                [jax.ShapeDtypeStruct((length, cols), t) for t in (jnp.float32, jnp.bfloat16)],
                {}, flops[c],
            )
            halves.append(half)
            received.append(shifted(sent, "replica", distance))
        for c, (at, length) in enumerate(pieces):
            ins = [mixed_weight, halves[c], received[c], tok, messages[c]] + carried
            specs = [spec_weight, spec_chunk, spec_chunk, spec_tok(at), spec_other(leads[c])]
            if carried:
                specs += [spec_mixed, spec_grads, spec_other_grads]
            carried = list(call(
                partial(mix_kernel, c == 0), length, ins, specs,
                [spec_rows(at), spec_grads, spec_other_grads], [shape_mixed] + shape_sums,
                {6: 0} if carried else {}, flops[c],
            ))

    mixed, sums, other_sums = carried
    other_sums = other_sums.astype(jnp.bfloat16)
    for step in range(1, shards):
        back = shifted(other_sums[(step - 1) * toks:step * toks], "shard", shards - step)
        sums = sums + back.astype(jnp.float32)
    return sums.astype(jnp.bfloat16)[None], mixed, mixed_weight


def per_device(tokens, key_grads, numerator, push_weight, train_step):
    replicas = lax.axis_size("replica")
    distances = [(1 << level) % replicas for level in range(5)]
    branches = [partial(branch, distance=distance) for distance in distances]
    return lax.switch(jnp.remainder(train_step, 5), branches, tokens, key_grads, numerator, push_weight)


def solution(mesh):
    return jax.shard_map(
        per_device,
        mesh=mesh,
        in_specs=(
            P("replica", "shard", None),
            P("replica", "shard", None),
            P("replica", "shard", None),
            P("replica"),
            P(),
        ),
        out_specs=(P("replica", "shard", None), P("replica", "shard", None), P("replica")),
        check_vma=False,
    )
```

```python
from functools import partial

import jax
import jax.numpy as jnp
from jax import lax
from jax.experimental import pallas as pl
from jax.experimental.pallas import tpu as pltpu
from jax.sharding import PartitionSpec as P

learn_rate = 0.5
extra = 16
params = pltpu.CompilerParams(vmem_limit_bytes=24 * 1024 * 1024)
vmem = pl.BlockSpec(memory_space=pltpu.VMEM)
smem = pl.BlockSpec(memory_space=pltpu.SMEM)
anywhere = pl.BlockSpec(memory_space=pl.ANY)
f32, bf16 = jnp.float32, jnp.bfloat16


def shifted(value, axis, by):
    count = lax.axis_size(axis)
    return lax.ppermute(value, axis, [(i, (i + by) % count) for i in range(count)])


def plan(rows, cols, distance):
    if rows != 2048:
        lengths = [rows // 2, rows // 2]
        return lengths, lengths, [1], [cols], [1]
    if distance == 0:
        return [768, 1024, 256], [768, 1024, 256], [1, 1], [cols], [1]
    if distance == 1:
        return [512, 768, 512, 256], [512, 768, 512, 256], [1, 2, 2], [cols], [1]
    return [512, 768, 768], [512, 512, 1024], [1, 1], [cols - 256, 128, 128], [2, 1]


def located(messages, chunks):
    out, m, used = [], 0, 0
    for length in chunks:
        pieces = []
        while length:
            size = min(length, messages[m] - used)
            pieces.append((m, used, size))
            used, length = used + size, length - size
            if used == messages[m]:
                m, used = m + 1, 0
        out.append(pieces)
    return out


def shape(dims, kind):
    return jax.ShapeDtypeStruct(dims, kind)


def call(kernel, ins, in_specs, outs, out_specs, micros, scratch=(), aliases={}):
    moved = int(micros * 3.5e6)
    return pl.pallas_call(
        kernel,
        in_specs=in_specs,
        out_specs=out_specs,
        out_shape=outs,
        scratch_shapes=scratch,
        input_output_aliases=aliases,
        compiler_params=params,
        cost_estimate=pl.CostEstimate(flops=0, bytes_accessed=moved, transcendentals=0),
    )(*ins)


def transposed_dot(a, b):
    return lax.dot_general(a, b, (((0,), (0,)), ((), ())), preferred_element_type=f32)


def step_of(rows):
    return 256 if rows % 256 == 0 else 128


def pack_kernel(rows, at, length, shards, lead, last, starts, scale, *refs):
    index, tok = refs[:2]
    grads = refs[2] if lead or last else None
    numerator = refs[3] if last else None
    outs = refs[2 + bool(lead or last) + bool(last) + (not lead):-1]
    sems = refs[-1]
    messages = outs[:shards - 1]
    copies = []

    def begin(src, dst):
        copy = pltpu.make_async_copy(src, dst, sems.at[len(copies)])
        copy.start()
        copies.append(copy)

    if last:
        own_tok = outs[shards - 1]
        bases = outs[shards:]
        begin(tok.at[:, pl.ds(pl.multiple_of(index[0] * rows, 128), rows)], own_tok)
    for step in range(1, shards):
        peer = lax.rem(index[0] + step, shards)
        part = tok.at[:, pl.ds(pl.multiple_of(peer * rows + at, 128), length)]
        begin(part, messages[step - 1].at[:, lead:])
        if lead:
            begin(grads, messages[step - 1].at[:, :lead])
    for copy in copies:
        copy.wait()
    if last:
        for base, (start, size) in zip(bases, starts):
            block = step_of(size)

            @pl.loop(0, size // block)
            def _(i):
                there = pl.ds(pl.multiple_of(start + i * block, 128), block)
                product = transposed_dot(own_tok[:, there], grads[...]).astype(bf16).astype(f32)
                here = pl.ds(pl.multiple_of(i * block, 128), block)
                base[here, :] = 0.5 * numerator[0, there, :] - scale * product


def blocks_of(pieces, lead, part):
    at = 0
    for k, (m, start, size) in enumerate(pieces):
        block = min(step_of(size), step_of(part))
        for i in range(size // block):
            yield k, (lead if m == 0 else 0) + start + i * block, at, block
            at += block


def update_kernel(scale, toks, cols, first, pieces, widths, *refs):
    refs = list(refs)
    weight = refs.pop(0) if first else None
    base = refs.pop(0)
    parts = [refs.pop(0) for _ in pieces]
    grads = parts[0] if first else refs.pop(0)
    if not first:
        refs.pop(0)
    half, *sends = refs
    part = base.shape[0] // len(sends) if sends and widths is None else base.shape[0]
    for k, col, at, block in blocks_of(pieces, cols, part):
        value = base[at:at + block, :]
        for j in range(parts[k].shape[0] // toks):
            own = slice(j * toks, (j + 1) * toks)
            product = transposed_dot(parts[k][own, col:col + block], grads[own, :cols])
            value -= scale * product.astype(bf16).astype(f32)
        half[at:at + block, :] = value
        if sends and widths is None:
            sends[at // part][at % part:at % part + block, :] = value.astype(bf16)
        elif sends:
            begin = 0
            for sent, width in zip(sends, widths):
                sent[at:at + block, :] = value[:, begin:begin + width].astype(bf16)
                begin += width

    if first and sends:
        length = base.shape[0]
        rest = jnp.full((extra, 128), 0.5 * weight[0], f32)
        for k in range(cols // 128):
            piece = rest.astype(bf16)
            sends[0][length:, k * 128:(k + 1) * 128] = piece
            rest -= piece.astype(f32)


def divided(value, row):
    inverse = 1.0 / row
    wide = jnp.concatenate([inverse] * (value.shape[1] // 128), axis=1)
    return (value * wide).astype(bf16)


def weight_row(weight, received, length, cols):
    own = jnp.full((1, 128), 0.5 * weight[0], f32)
    if received is None:
        return own + own
    piece = received[length:, :].astype(f32)[:1]
    total = piece[:, :128]
    for k in range(1, cols // 128):
        total += piece[:, k * 128:(k + 1) * 128]
    return own + total


def matched_dot(parts, pieces, lead, debiased):
    at, total = 0, None
    for part, (m, start, size) in zip(parts, pieces):
        col = (lead if m == 0 else 0) + start
        product = jnp.dot(part[:, col:col + size], debiased[at:at + size, :], preferred_element_type=f32)
        total = product if total is None else total + product
        at += size
    return total


def mix_kernel(at, first, cols, pieces, arrivals, *refs):
    refs = list(refs)
    weight, half = refs.pop(0), refs.pop(0)
    received = [refs.pop(0) for _ in range(arrivals)]
    own_tok = refs.pop(0)
    parts = [refs.pop(0) for _ in pieces]
    length = half.shape[0]
    if first:
        mixed, sums, other_sums, row_out, weight_out, value_ref, debiased, sem = refs
        row = weight_row(weight, received[0] if received else None, length, cols)
        row_out[...] = jnp.broadcast_to(row, row_out.shape)
        weight_out[0] = jnp.max(row)
    else:
        sums_in, other_in, _, mixed, sums, other_sums, value_ref, debiased, sem = refs
        row = weight[:1, :]
    size = length // max(1, len(received))
    block = step_of(size)
    for i in range(0, length, block):
        value = half[i:i + block, :]
        if received:
            value += received[i // size][i % size:i % size + block, :].astype(f32)
        else:
            value += value
        value_ref[i:i + block, :] = value
        debiased[i:i + block, :] = divided(value, row)

    copy = pltpu.make_async_copy(value_ref, mixed.at[0, pl.ds(at, length), :], sem)
    copy.start()
    own = jnp.dot(own_tok[:, at:at + length], debiased[...], preferred_element_type=f32)
    other = matched_dot(parts, pieces, cols, debiased)
    if first:
        sums[...] = own
        other_sums[...] = other
    else:
        sums[...] = sums_in[...] + own
        other_sums[...] = other_in[...] + other
    copy.wait()


def last_value(half, received, i, block, begin, width):
    value = half[i:i + block, begin:begin + width]
    if not received:
        return value + value
    arrived = [part[i:i + block, :].astype(f32) for part in received]
    return value + (arrived[0] if len(arrived) == 1 else jnp.concatenate(arrived, axis=1))


def last_other_kernel(begin, width, cols, pieces, arrivals, *refs):
    refs = list(refs)
    row, half = refs.pop(0), refs.pop(0)
    received = [refs.pop(0) for _ in range(arrivals)]
    parts = [refs.pop(0) for _ in pieces]
    before, _, out, debiased = refs
    length = half.shape[0]
    block = step_of(length)
    for i in range(0, length, block):
        debiased[i:i + block, :] = divided(last_value(half, received, i, block, begin, width), row[:1, :])
    other = matched_dot(parts, pieces, cols, debiased)
    out[...] = (before[:, begin:begin + width] + other).astype(bf16)


def last_own_kernel(at, begin, width, arrivals, *refs):
    refs = list(refs)
    row, half = refs.pop(0), refs.pop(0)
    received = [refs.pop(0) for _ in range(arrivals)]
    own_tok, before, _, mixed, out, value_ref, debiased, sem = refs
    length = half.shape[0]
    block = step_of(length)
    for i in range(0, length, block):
        value = last_value(half, received, i, block, begin, width)
        value_ref[i:i + block, :] = value
        debiased[i:i + block, :] = divided(value, row[:1, :])
    copy = pltpu.make_async_copy(
        value_ref, mixed.at[0, pl.ds(at, length), pl.ds(begin, width)], sem
    )
    copy.start()
    own = jnp.dot(own_tok[:, at:at + length], debiased[...], preferred_element_type=f32)
    out[...] = before[:, begin:begin + width] + own
    copy.wait()


def keys_kernel(groups, count, *refs):
    out = refs[-1]
    at = 0
    for g, width in enumerate(groups):
        value = refs[g][...]
        for k in range(count):
            value += refs[len(groups) + g * count + k][...].astype(f32)
        out[0, :, at:at + width] = value.astype(bf16)
        at += width


def branch(tokens, key_grads, numerator, push_weight, distance):
    shards = lax.axis_size("shard")
    index = lax.axis_index("shard").astype(jnp.int32)[None]
    tok, grads = tokens[0], key_grads[0]
    toks, cols = grads.shape
    rows = numerator.shape[1]
    total = toks * shards
    others = (shards - 1) * toks
    message_rows, lengths, part_counts, widths, group_sizes = plan(rows, cols, distance)
    starts = [(sum(lengths[:c]), length) for c, length in enumerate(lengths)]
    pieces = located(message_rows, lengths)
    scale = 0.5 * learn_rate / total
    moves = distance != 0
    dma = pltpu.SemaphoreType.DMA

    sent, previous = [], None
    for m, length in enumerate(message_rows):
        last = m == len(message_rows) - 1
        lead = cols if m == 0 else 0
        ins, specs = [index, tok], [smem, anywhere]
        if lead or last:
            ins.append(grads)
            specs.append(vmem if last else anywhere)
        if last:
            ins.append(numerator)
            specs.append(vmem)
        if not lead:
            ins.append(previous)
            specs.append(anywhere)
        outs = [shape((toks, lead + length), bf16)] * (shards - 1)
        if last:
            outs = outs + [shape((toks, rows), bf16)] + [shape((size, cols), f32) for _, size in starts]
        results = call(
            partial(pack_kernel, rows, sum(message_rows[:m]), length, shards, lead, last, starts, scale),
            ins, specs, outs, [vmem] * len(outs), 3 if last else 1,
            scratch=[dma((2 * shards,))],
        )
        previous = results[0]
        sent.append(results[:shards - 1])
        if last:
            own_tok, bases = results[shards - 1], results[shards:]
    messages = []
    for parts in sent:
        arrived = [shifted(part, "shard", step) for step, part in enumerate(parts, 1)]
        messages.append(arrived[0] if shards == 2 else jnp.concatenate(arrived, axis=0))

    halves, received = [], []
    for c, (at, length) in enumerate(starts):
        first, last = c == 0, c == len(starts) - 1
        parts = [messages[m] for m, _, _ in pieces[c]]
        if first:
            ins = [push_weight, bases[c]] + parts
            specs = [smem] + [vmem] * (len(ins) - 1)
        else:
            ins = [bases[c]] + parts + [messages[0], halves[-1]]
            specs = [vmem] * (len(ins) - 1) + [anywhere]
        outs = [shape((length, cols), f32)]
        if moves and last:
            outs += [shape((length, width), bf16) for width in widths]
        elif moves:
            size = length // part_counts[c]
            outs += [shape((size + (extra if first else 0), cols), bf16)] * (length // size)
        half, *sends = call(
            partial(update_kernel, scale, toks, cols, first, pieces[c], widths if last else None),
            ins, specs, outs, [vmem] * len(outs), 1,
        )
        halves.append(half)
        received.append([shifted(part, "replica", distance) for part in sends])

    shape_mixed = shape(numerator.shape, f32)
    shape_sums = [shape((toks, cols), f32), shape((others, cols), f32)]
    row = mixed = sums = other_sums = mixed_weight = None
    for c, (at, length) in enumerate(starts[:-1]):
        first = c == 0
        parts = [messages[m] for m, _, _ in pieces[c]]
        ins = [push_weight if first else row, halves[c]] + received[c] + [own_tok] + parts
        specs = [smem if first else vmem] + [vmem] * (len(ins) - 1)
        outs, out_specs = [shape_mixed] + shape_sums, [anywhere, vmem, vmem]
        if first:
            outs = outs + [shape((8, 128), f32), shape((1,), f32)]
            out_specs = out_specs + [vmem, smem]
        else:
            ins += [sums, other_sums, mixed]
            specs += [vmem, vmem, anywhere]
        results = call(
            partial(mix_kernel, at, first, cols, pieces[c], len(received[c])), ins, specs, outs, out_specs,
            4, scratch=[pltpu.VMEM((length, cols), f32), pltpu.VMEM((length, cols), bf16), dma(())],
            aliases={} if first else {len(ins) - 1: 0},
        )
        mixed, sums, other_sums = results[:3]
        if first:
            row, mixed_weight = results[3:]

    at, length = starts[-1]
    parts = [messages[m] for m, _, _ in pieces[-1]]
    groups, own_parts, back_parts, begin, done = [], [], [], 0, 0
    for count in group_sizes:
        width = sum(widths[done:done + count])
        arrived = received[-1][done:done + count]
        ins = [row, halves[-1]] + arrived + parts + [other_sums, mixed]
        other = call(
            partial(last_other_kernel, begin, width, cols, pieces[-1], len(arrived)),
            ins, [vmem] * (len(ins) - 1) + [anywhere], [shape((others, width), bf16)], [vmem],
            1, scratch=[pltpu.VMEM((length, width), bf16)],
        )[0]
        for step in range(1, shards):
            back_parts.append(shifted(other[(step - 1) * toks:step * toks], "shard", shards - step))
        ins = [row, halves[-1]] + arrived + [own_tok, sums, mixed]
        mixed, own = call(
            partial(last_own_kernel, at, begin, width, len(arrived)),
            ins, [vmem] * (len(ins) - 1) + [anywhere], [shape_mixed, shape((toks, width), f32)],
            [anywhere, vmem], 2,
            scratch=[pltpu.VMEM((length, width), f32), pltpu.VMEM((length, width), bf16), dma(())],
            aliases={len(ins) - 1: 0},
        )
        own_parts.append(own)
        groups.append(width)
        begin, done = begin + width, done + count
    keys = call(
        partial(keys_kernel, groups, shards - 1), own_parts + back_parts,
        [vmem] * (len(own_parts) + len(back_parts)), [shape((1, toks, cols), bf16)], [vmem], 0.1,
    )[0]
    return keys, mixed, mixed_weight


def per_device(tokens, key_grads, numerator, push_weight, train_step):
    replicas = lax.axis_size("replica")
    distances = [(1 << level) % replicas for level in range(5)]
    branches = [partial(branch, distance=distance) for distance in distances]
    return lax.switch(lax.rem(train_step, 5), branches, tokens, key_grads, numerator, push_weight)


def solution(mesh):
    return jax.shard_map(
        per_device,
        mesh=mesh,
        in_specs=(
            P("replica", "shard", None),
            P("replica", "shard", None),
            P("replica", "shard", None),
            P("replica"),
            P(),
        ),
        out_specs=(P("replica", "shard", None), P("replica", "shard", None), P("replica")),
        check_vma=False,
    )
```

```python
from functools import partial

import jax
import jax.numpy as jnp
from jax import lax
from jax.experimental import pallas as pl
from jax.experimental.pallas import tpu as pltpu
from jax.sharding import PartitionSpec as P

learn_rate = 0.5
extra = 16
params = pltpu.CompilerParams(vmem_limit_bytes=24 * 1024 * 1024)
vmem = pl.BlockSpec(memory_space=pltpu.VMEM)
smem = pl.BlockSpec(memory_space=pltpu.SMEM)
anywhere = pl.BlockSpec(memory_space=pl.ANY)
f32, bf16 = jnp.float32, jnp.bfloat16


def shifted(value, axis, by):
    count = lax.axis_size(axis)
    return lax.ppermute(value, axis, [(i, (i + by) % count) for i in range(count)])


def plan(rows, cols, distance):
    if rows != 2048:
        lengths = [rows // 2, rows // 2]
        return lengths, lengths, [1], [cols], [1]
    if distance == 0:
        return [512] * 4, [512] * 4, [1] * 3, [cols], [1]
    if distance == 1:
        return [512] * 4, [512] * 4, [1, 1, 1], [cols // 2, cols // 2], [1, 1]
    return [384, 384, 640, 640], [384, 384, 1280], [1, 1], [128] * (cols // 128), [cols // 128 - 1, 1]


def located(messages, chunks):
    out, m, used = [], 0, 0
    for length in chunks:
        pieces = []
        while length:
            size = min(length, messages[m] - used)
            pieces.append((m, used, size))
            used, length = used + size, length - size
            if used == messages[m]:
                m, used = m + 1, 0
        out.append(pieces)
    return out


def shape(dims, kind):
    return jax.ShapeDtypeStruct(dims, kind)


def call(kernel, ins, in_specs, outs, out_specs, micros, scratch=(), aliases={}):
    moved = int(micros * 3.5e6)
    return pl.pallas_call(
        kernel,
        in_specs=in_specs,
        out_specs=out_specs,
        out_shape=outs,
        scratch_shapes=scratch,
        input_output_aliases=aliases,
        compiler_params=params,
        cost_estimate=pl.CostEstimate(flops=0, bytes_accessed=moved, transcendentals=0),
    )(*ins)


def transposed_dot(a, b):
    return lax.dot_general(a, b, (((0,), (0,)), ((), ())), preferred_element_type=f32)


def step_of(rows):
    return 256 if rows % 256 == 0 else 128


def pack_kernel(rows, at, length, shards, *refs):
    index, tok = refs[:2]
    *messages, sems = refs[-shards:]
    copies = []
    for step in range(1, shards):
        peer = lax.rem(index[0] + step, shards)
        part = tok.at[:, pl.ds(pl.multiple_of(peer * rows + at, 128), length)]
        copy = pltpu.make_async_copy(part, messages[step - 1], sems.at[step - 1])
        copy.start()
        copies.append(copy)
    for copy in copies:
        copy.wait()


def base_kernel(rows, starts, scale, index, tok, grads, numerator, _, own_tok, *refs):
    *bases, sem = refs
    copy = pltpu.make_async_copy(
        tok.at[:, pl.ds(pl.multiple_of(index[0] * rows, 128), rows)], own_tok, sem
    )
    copy.start()
    copy.wait()
    for base, (start, size) in zip(bases, starts):
        block = step_of(size)

        @pl.loop(0, size // block)
        def _(i):
            there = pl.ds(pl.multiple_of(start + i * block, 128), block)
            product = transposed_dot(own_tok[:, there], grads[...]).astype(bf16).astype(f32)
            here = pl.ds(pl.multiple_of(i * block, 128), block)
            base[here, :] = 0.5 * numerator[0, there, :] - scale * product


def blocks_of(pieces, part):
    at = 0
    for k, (_, start, size) in enumerate(pieces):
        block = min(step_of(size), step_of(part))
        for i in range(size // block):
            yield k, start + i * block, at, block
            at += block


def copy_kernel(source, _, target):
    target[...] = source[...]


def update_kernel(scale, toks, first, pieces, widths, *refs):
    refs = list(refs)
    weight = refs.pop(0) if first else None
    base = refs.pop(0)
    parts = [refs.pop(0) for _ in pieces]
    grads = refs.pop(0)
    if not first:
        refs.pop(0)
    half, *sends = refs
    part = base.shape[0] // len(sends) if sends and widths is None else base.shape[0]
    for k, col, at, block in blocks_of(pieces, part):
        value = base[at:at + block, :]
        for j in range(parts[k].shape[0] // toks):
            own = slice(j * toks, (j + 1) * toks)
            product = transposed_dot(parts[k][own, col:col + block], grads[own, :])
            value -= scale * product.astype(bf16).astype(f32)
        half[at:at + block, :] = value
        if sends and widths is None:
            sends[at // part][at % part:at % part + block, :] = value.astype(bf16)
        elif sends:
            begin = 0
            for sent, width in zip(sends, widths):
                sent[at:at + block, :] = value[:, begin:begin + width].astype(bf16)
                begin += width

    if first and sends:
        length = base.shape[0]
        rest = jnp.full((extra, 128), 0.5 * weight[0], f32)
        for k in range(sends[0].shape[1] // 128):
            piece = rest.astype(bf16)
            sends[0][length:, k * 128:(k + 1) * 128] = piece
            rest -= piece.astype(f32)


def divided(value, row):
    inverse = 1.0 / row
    wide = jnp.concatenate([inverse] * (value.shape[1] // 128), axis=1)
    return (value * wide).astype(bf16)


def weight_row(weight, received, length, cols):
    own = jnp.full((1, 128), 0.5 * weight[0], f32)
    if received is None:
        return own + own
    piece = received[length:, :].astype(f32)[:1]
    total = piece[:, :128]
    for k in range(1, cols // 128):
        total += piece[:, k * 128:(k + 1) * 128]
    return own + total


def matched_dot(parts, pieces, debiased):
    at, total = 0, None
    for part, (_, start, size) in zip(parts, pieces):
        product = jnp.dot(part[:, start:start + size], debiased[at:at + size, :], preferred_element_type=f32)
        total = product if total is None else total + product
        at += size
    return total


def mix_kernel(at, first, cols, pieces, arrivals, *refs):
    refs = list(refs)
    weight, half = refs.pop(0), refs.pop(0)
    received = [refs.pop(0) for _ in range(arrivals)]
    own_tok = refs.pop(0)
    parts = [refs.pop(0) for _ in pieces]
    length = half.shape[0]
    if first:
        mixed, sums, other_sums, row_out, weight_out, value_ref, debiased, sem = refs
        row = weight_row(weight, received[0] if received else None, length, cols)
        row_out[...] = jnp.broadcast_to(row, row_out.shape)
        weight_out[0] = jnp.max(row)
    else:
        sums_in, other_in, _, mixed, sums, other_sums, value_ref, debiased, sem = refs
        row = weight[:1, :]
    size = length // max(1, len(received))
    block = step_of(size)
    for i in range(0, length, block):
        value = half[i:i + block, :]
        if received:
            value += received[i // size][i % size:i % size + block, :].astype(f32)
        else:
            value += value
        value_ref[i:i + block, :] = value
        debiased[i:i + block, :] = divided(value, row)

    copy = pltpu.make_async_copy(value_ref, mixed.at[0, pl.ds(at, length), :], sem)
    copy.start()
    own = jnp.dot(own_tok[:, at:at + length], debiased[...], preferred_element_type=f32)
    other = matched_dot(parts, pieces, debiased)
    if first:
        sums[...] = own
        other_sums[...] = other
    else:
        sums[...] = sums_in[...] + own
        other_sums[...] = other_in[...] + other
    copy.wait()


def last_value(half, received, i, block, begin, width):
    value = half[i:i + block, begin:begin + width]
    if not received:
        return value + value
    arrived = [part[i:i + block, :].astype(f32) for part in received]
    return value + (arrived[0] if len(arrived) == 1 else jnp.concatenate(arrived, axis=1))


def last_other_kernel(begin, width, pieces, arrivals, *refs):
    refs = list(refs)
    row, half = refs.pop(0), refs.pop(0)
    received = [refs.pop(0) for _ in range(arrivals)]
    parts = [refs.pop(0) for _ in pieces]
    before, out, debiased = refs[0], refs[-2], refs[-1]
    length = half.shape[0]
    block = step_of(length)
    for i in range(0, length, block):
        debiased[i:i + block, :] = divided(last_value(half, received, i, block, begin, width), row[:1, :])
    other = matched_dot(parts, pieces, debiased)
    out[...] = (before[:, begin:begin + width] + other).astype(bf16)


def last_own_kernel(at, begin, width, arrivals, *refs):
    refs = list(refs)
    row, half = refs.pop(0), refs.pop(0)
    received = [refs.pop(0) for _ in range(arrivals)]
    own_tok, before, _, mixed, out, value_ref, debiased, sem = refs
    length = half.shape[0]
    block = step_of(length)
    for i in range(0, length, block):
        value = last_value(half, received, i, block, begin, width)
        value_ref[i:i + block, :] = value
        debiased[i:i + block, :] = divided(value, row[:1, :])
    copy = pltpu.make_async_copy(
        value_ref, mixed.at[0, pl.ds(at, length), pl.ds(begin, width)], sem
    )
    copy.start()
    own = jnp.dot(own_tok[:, at:at + length], debiased[...], preferred_element_type=f32)
    out[...] = before[:, begin:begin + width] + own
    copy.wait()


def keys_kernel(groups, count, *refs):
    keys, out, sem = refs[-3:]
    at = 0
    for g, width in enumerate(groups):
        value = refs[g][...]
        for k in range(count):
            value += refs[len(groups) + g * count + k][...].astype(f32)
        out[0, :, at:at + width] = value.astype(bf16)
        at += width
    copy = pltpu.make_async_copy(out, keys, sem)
    copy.start()
    copy.wait()


def branch(tokens, key_grads, numerator, push_weight, distance):
    shards = lax.axis_size("shard")
    index = lax.axis_index("shard").astype(jnp.int32)[None]
    tok, grads = tokens[0], key_grads[0]
    toks, cols = grads.shape
    rows = numerator.shape[1]
    total = toks * shards
    others = (shards - 1) * toks
    message_rows, lengths, part_counts, widths, group_sizes = plan(rows, cols, distance)
    starts = [(sum(lengths[:c]), length) for c, length in enumerate(lengths)]
    pieces = located(message_rows, lengths)
    scale = 0.5 * learn_rate / total
    moves = distance != 0
    dma = pltpu.SemaphoreType.DMA

    def joined(parts):
        arrived = [shifted(part, "shard", step) for step, part in enumerate(parts, 1)]
        return arrived[0] if shards == 2 else jnp.concatenate(arrived, axis=0)

    def packed(m, waits):
        at = sum(message_rows[:m])
        return call(
            partial(pack_kernel, rows, at, message_rows[m], shards),
            [index, tok] + waits, [smem] + [anywhere] * (1 + len(waits)),
            [shape((toks, message_rows[m]), bf16)] * (shards - 1), [vmem] * (shards - 1), 1,
            scratch=[dma((shards,))],
        )

    parts = packed(0, [])
    own_tok, *bases = call(
        partial(base_kernel, rows, starts, scale),
        [index, tok, grads, numerator, parts[0]], [smem, anywhere, vmem, vmem, anywhere],
        [shape((toks, rows), bf16)] + [shape((size, cols), f32) for _, size in starts],
        [vmem] * (1 + len(starts)), 3, scratch=[dma(())],
    )
    other_grads = joined([grads] * (shards - 1))
    other_grads = call(
        copy_kernel, [other_grads, bases[0]], [vmem, anywhere], [shape((others, cols), bf16)], [vmem], 0.2
    )[0]
    messages = [joined(parts)]

    shape_mixed = shape(numerator.shape, f32)
    shape_sums = [shape((toks, cols), f32), shape((others, cols), f32)]
    halves, received, state = [], [], {}

    def update(c):
        at, length = starts[c]
        first, last = c == 0, c == len(starts) - 1
        parts = [messages[m] for m, _, _ in pieces[c]]
        if first:
            ins = [push_weight, bases[c]] + parts + [other_grads]
            specs = [smem] + [vmem] * (len(ins) - 1)
        else:
            ins = [bases[c]] + parts + [other_grads, state.get("sums", halves[-1])]
            specs = [vmem] * (len(ins) - 1) + [anywhere]
        outs = [shape((length, cols), f32)]
        if moves and last:
            outs += [shape((length, width), bf16) for width in widths]
        elif moves:
            size = length // part_counts[c]
            outs += [shape((size + (extra if first else 0), cols), bf16)] * (length // size)
        half, *sends = call(
            partial(update_kernel, scale, toks, first, pieces[c], widths if last else None),
            ins, specs, outs, [vmem] * len(outs), 1,
        )
        halves.append(half)
        received.append([shifted(part, "replica", distance) for part in sends])

    def mix(c):
        at, length = starts[c]
        first = c == 0
        parts = [messages[m] for m, _, _ in pieces[c]]
        ins = [push_weight if first else state["row"], halves[c]] + received[c] + [own_tok] + parts
        specs = [smem if first else vmem] + [vmem] * (len(ins) - 1)
        outs, out_specs = [shape_mixed] + shape_sums, [anywhere, vmem, vmem]
        if first:
            outs = outs + [shape((8, 128), f32), shape((1,), f32)]
            out_specs = out_specs + [vmem, smem]
        else:
            ins += [state["sums"], state["other"], state["mixed"]]
            specs += [vmem, vmem, anywhere]
        results = call(
            partial(mix_kernel, at, first, cols, pieces[c], len(received[c])), ins, specs, outs, out_specs,
            4, scratch=[pltpu.VMEM((length, cols), f32), pltpu.VMEM((length, cols), bf16), dma(())],
            aliases={} if first else {len(ins) - 1: 0},
        )
        state.update(zip(["mixed", "sums", "other", "row", "weight"], results))

    for c in range(len(starts)):
        for m in range(len(messages), pieces[c][-1][0] + 1):
            if distance <= 1:
                waits = [parts[0]]
            else:
                waits = [other_grads] if m == 1 else [halves[min(m - 2, c - 1)]]
            parts = packed(m, waits)
            messages.append(joined(parts))
        early = c - 2 if distance > 1 else (c - 1 if not moves else -1)
        if early >= 0:
            mix(early)
        update(c)
    for c in range(early + 1, len(starts) - 1):
        mix(c)
    mixed, sums, other_sums, row, mixed_weight = [state[k] for k in ["mixed", "sums", "other", "row", "weight"]]

    at, length = starts[-1]
    chunk_parts = [messages[m] for m, _, _ in pieces[-1]]
    groups, own_parts, back_parts, begin, done = [], [], [], 0, 0
    for count in group_sizes:
        width = sum(widths[done:done + count])
        arrived = received[-1][done:done + count]
        ins = [row, halves[-1]] + arrived + chunk_parts + [other_sums, mixed]
        other = call(
            partial(last_other_kernel, begin, width, pieces[-1], len(arrived)),
            ins, [vmem] * (len(ins) - 1) + [anywhere],
            [shape((others, width), bf16)], [vmem],
            1, scratch=[pltpu.VMEM((length, width), bf16)],
        )[0]
        for step in range(1, shards):
            back_parts.append(shifted(other[(step - 1) * toks:step * toks], "shard", shards - step))
        ins = [row, halves[-1]] + arrived + [own_tok, sums, mixed]
        mixed, own = call(
            partial(last_own_kernel, at, begin, width, len(arrived)),
            ins, [vmem] * (len(ins) - 1) + [anywhere], [shape_mixed, shape((toks, width), f32)],
            [anywhere, vmem], 2,
            scratch=[pltpu.VMEM((length, width), f32), pltpu.VMEM((length, width), bf16), dma(())],
            aliases={len(ins) - 1: 0},
        )
        own_parts.append(own)
        groups.append(width)
        begin, done = begin + width, done + count
    keys = call(
        partial(keys_kernel, groups, shards - 1), own_parts + back_parts,
        [vmem] * (len(own_parts) + len(back_parts)), [shape((1, toks, cols), bf16)], [anywhere], 0.1,
        scratch=[pltpu.VMEM((1, toks, cols), bf16), dma(())],
    )[0]
    return keys, mixed, mixed_weight


def per_device(tokens, key_grads, numerator, push_weight, train_step):
    replicas = lax.axis_size("replica")
    distances = [(1 << level) % replicas for level in range(5)]
    branches = [partial(branch, distance=distance) for distance in distances]
    return lax.switch(lax.rem(train_step, 5), branches, tokens, key_grads, numerator, push_weight)


def solution(mesh):
    return jax.shard_map(
        per_device,
        mesh=mesh,
        in_specs=(
            P("replica", "shard", None),
            P("replica", "shard", None),
            P("replica", "shard", None),
            P("replica"),
            P(),
        ),
        out_specs=(P("replica", "shard", None), P("replica", "shard", None), P("replica")),
        check_vma=False,
    )
```

```python
from functools import partial

import jax
import jax.numpy as jnp
from jax import lax
from jax.experimental import pallas as pl
from jax.experimental.pallas import tpu as pltpu
from jax.sharding import PartitionSpec as P

learn_rate = 0.5
extra = 16
params = pltpu.CompilerParams(vmem_limit_bytes=24 * 1024 * 1024)
vmem = pl.BlockSpec(memory_space=pltpu.VMEM)
smem = pl.BlockSpec(memory_space=pltpu.SMEM)
anywhere = pl.BlockSpec(memory_space=pl.ANY)
f32, bf16 = jnp.float32, jnp.bfloat16


def shifted(value, axis, by):
    count = lax.axis_size(axis)
    return lax.ppermute(value, axis, [(i, (i + by) % count) for i in range(count)])


def plan(rows, cols, distance):
    if rows != 2048:
        lengths = [rows // 2, rows // 2]
        return lengths, lengths, [1], [cols], [1]
    if distance == 0:
        return [512] * 4, [512] * 4, [1] * 3, [cols], [1]
    if distance == 1:
        return [512] * 4, [512] * 4, [1, 1, 1], [cols // 2, cols // 2], [1, 1]
    return [384, 384, 640, 640], [384, 384, 256, 1024], [1, 1, 1], [128] * (cols // 128), [cols // 128 - 1, 1]


def located(messages, chunks):
    out, m, used = [], 0, 0
    for length in chunks:
        pieces = []
        while length:
            size = min(length, messages[m] - used)
            pieces.append((m, used, size))
            used, length = used + size, length - size
            if used == messages[m]:
                m, used = m + 1, 0
        out.append(pieces)
    return out


def shape(dims, kind):
    return jax.ShapeDtypeStruct(dims, kind)


def call(kernel, ins, in_specs, outs, out_specs, micros, scratch=(), aliases={}):
    moved = int(micros * 3.5e6)
    return pl.pallas_call(
        kernel,
        in_specs=in_specs,
        out_specs=out_specs,
        out_shape=outs,
        scratch_shapes=scratch,
        input_output_aliases=aliases,
        compiler_params=params,
        cost_estimate=pl.CostEstimate(flops=0, bytes_accessed=moved, transcendentals=0),
    )(*ins)


def transposed_dot(a, b):
    return lax.dot_general(a, b, (((0,), (0,)), ((), ())), preferred_element_type=f32)


def step_of(rows):
    return 256 if rows % 256 == 0 else 128


def pack_kernel(rows, at, length, shards, *refs):
    index, tok = refs[:2]
    *messages, sems = refs[-shards:]
    copies = []
    for step in range(1, shards):
        peer = lax.rem(index[0] + step, shards)
        part = tok.at[:, pl.ds(pl.multiple_of(peer * rows + at, 128), length)]
        copy = pltpu.make_async_copy(part, messages[step - 1], sems.at[step - 1])
        copy.start()
        copies.append(copy)
    for copy in copies:
        copy.wait()


def base_kernel(rows, starts, scale, index, weight, tok, grads, numerator, _, own_tok, own_row, rows_out, *refs):
    *bases, sem = refs
    copy = pltpu.make_async_copy(
        tok.at[:, pl.ds(pl.multiple_of(index[0] * rows, 128), rows)], own_tok, sem
    )
    copy.start()
    own_row[...] = jnp.full(own_row.shape, 0.5 * weight[0], f32)
    rest = jnp.full((extra, 128), 0.5 * weight[0], f32)
    for k in range(rows_out.shape[1] // 128):
        piece = rest.astype(bf16)
        rows_out[:, k * 128:(k + 1) * 128] = piece
        rest -= piece.astype(f32)
    copy.wait()
    for base, (start, size) in zip(bases, starts):
        block = step_of(size)

        @pl.loop(0, size // block)
        def _(i):
            there = pl.ds(pl.multiple_of(start + i * block, 128), block)
            product = transposed_dot(own_tok[:, there], grads[...]).astype(bf16).astype(f32)
            here = pl.ds(pl.multiple_of(i * block, 128), block)
            base[here, :] = 0.5 * numerator[0, there, :] - scale * product


def blocks_of(pieces, part):
    at = 0
    for k, (_, start, size) in enumerate(pieces):
        block = min(step_of(size), step_of(part))
        for i in range(size // block):
            yield k, start + i * block, at, block
            at += block


def copy_kernel(source, _, target):
    target[...] = source[...]


def update_kernel(scale, toks, first, pieces, widths, *refs):
    refs = list(refs)
    weight_rows = refs.pop(0) if first else None
    base = refs.pop(0)
    parts = [refs.pop(0) for _ in pieces]
    grads = refs.pop(0)
    if not first:
        refs.pop(0)
    half, *sends = refs
    part = base.shape[0] // len(sends) if sends and widths is None else base.shape[0]
    for k, col, at, block in blocks_of(pieces, part):
        value = base[at:at + block, :]
        for j in range(parts[k].shape[0] // toks):
            own = slice(j * toks, (j + 1) * toks)
            product = transposed_dot(parts[k][own, col:col + block], grads[own, :])
            value -= scale * product.astype(bf16).astype(f32)
        half[at:at + block, :] = value
        if sends and widths is None:
            sends[at // part][at % part:at % part + block, :] = value.astype(bf16)
        elif sends:
            begin = 0
            for sent, width in zip(sends, widths):
                sent[at:at + block, :] = value[:, begin:begin + width].astype(bf16)
                begin += width

    if first and sends:
        sends[0][base.shape[0]:, :] = weight_rows[...]


def divided(value, row):
    inverse = 1.0 / row
    wide = jnp.concatenate([inverse] * (value.shape[1] // 128), axis=1)
    return (value * wide).astype(bf16)


def weight_row(own_row, received, length):
    own = own_row[:1, :]
    if received is None:
        return own + own
    piece = received[length:, :].astype(f32)[:1]
    total = piece[:, :128]
    for k in range(1, piece.shape[1] // 128):
        total += piece[:, k * 128:(k + 1) * 128]
    return own + total


def matched_dot(parts, pieces, debiased):
    at, total = 0, None
    for part, (_, start, size) in zip(parts, pieces):
        product = jnp.dot(part[:, start:start + size], debiased[at:at + size, :], preferred_element_type=f32)
        total = product if total is None else total + product
        at += size
    return total


def mix_kernel(at, first, cols, pieces, arrivals, *refs):
    refs = list(refs)
    weight, half = refs.pop(0), refs.pop(0)
    received = [refs.pop(0) for _ in range(arrivals)]
    own_tok = refs.pop(0)
    parts = [refs.pop(0) for _ in pieces]
    length = half.shape[0]
    if first:
        mixed, sums, other_sums, row_out, value_ref, debiased, sem = refs
        row = weight_row(weight, received[0] if received else None, length)
        row_out[...] = jnp.broadcast_to(row, row_out.shape)
    else:
        sums_in, other_in, _, mixed, sums, other_sums, value_ref, debiased, sem = refs
        row = weight[:1, :]
    size = length // max(1, len(received))
    block = step_of(size)
    for i in range(0, length, block):
        value = half[i:i + block, :]
        if received:
            value += received[i // size][i % size:i % size + block, :].astype(f32)
        else:
            value += value
        value_ref[i:i + block, :] = value
        debiased[i:i + block, :] = divided(value, row)

    copy = pltpu.make_async_copy(value_ref, mixed.at[0, pl.ds(at, length), :], sem)
    copy.start()
    own = jnp.dot(own_tok[:, at:at + length], debiased[...], preferred_element_type=f32)
    other = matched_dot(parts, pieces, debiased)
    if first:
        sums[...] = own
        other_sums[...] = other
    else:
        sums[...] = sums_in[...] + own
        other_sums[...] = other_in[...] + other
    copy.wait()


def last_value(half, received, i, block, begin, width):
    value = half[i:i + block, begin:begin + width]
    if not received:
        return value + value
    arrived = [part[i:i + block, :].astype(f32) for part in received]
    return value + (arrived[0] if len(arrived) == 1 else jnp.concatenate(arrived, axis=1))


def last_other_kernel(begin, width, pieces, arrivals, *refs):
    refs = list(refs)
    row, half = refs.pop(0), refs.pop(0)
    received = [refs.pop(0) for _ in range(arrivals)]
    parts = [refs.pop(0) for _ in pieces]
    before, out, debiased = refs[0], refs[-2], refs[-1]
    length = half.shape[0]
    block = step_of(length)
    for i in range(0, length, block):
        debiased[i:i + block, :] = divided(last_value(half, received, i, block, begin, width), row[:1, :])
    other = matched_dot(parts, pieces, debiased)
    out[...] = (before[:, begin:begin + width] + other).astype(bf16)


def last_own_kernel(at, begin, width, arrivals, *refs):
    refs = list(refs)
    row, half = refs.pop(0), refs.pop(0)
    received = [refs.pop(0) for _ in range(arrivals)]
    own_tok, before, _, mixed, out, *weight_out, value_ref, debiased, sem = refs
    if weight_out:
        weight_out[0][0] = jnp.max(row[:1, :])
    length = half.shape[0]
    block = step_of(length)
    for i in range(0, length, block):
        value = last_value(half, received, i, block, begin, width)
        value_ref[i:i + block, :] = value
        debiased[i:i + block, :] = divided(value, row[:1, :])
    copy = pltpu.make_async_copy(
        value_ref, mixed.at[0, pl.ds(at, length), pl.ds(begin, width)], sem
    )
    copy.start()
    own = jnp.dot(own_tok[:, at:at + length], debiased[...], preferred_element_type=f32)
    out[...] = before[:, begin:begin + width] + own
    copy.wait()


def keys_kernel(groups, count, *refs):
    keys, out, sem = refs[-3:]
    at = 0
    for g, width in enumerate(groups):
        value = refs[g][...]
        for k in range(count):
            value += refs[len(groups) + g * count + k][...].astype(f32)
        out[0, :, at:at + width] = value.astype(bf16)
        at += width
    copy = pltpu.make_async_copy(out, keys, sem)
    copy.start()
    copy.wait()


def branch(tokens, key_grads, numerator, push_weight, distance):
    shards = lax.axis_size("shard")
    index = lax.axis_index("shard").astype(jnp.int32)[None]
    tok, grads = tokens[0], key_grads[0]
    toks, cols = grads.shape
    rows = numerator.shape[1]
    total = toks * shards
    others = (shards - 1) * toks
    message_rows, lengths, part_counts, widths, group_sizes = plan(rows, cols, distance)
    starts = [(sum(lengths[:c]), length) for c, length in enumerate(lengths)]
    pieces = located(message_rows, lengths)
    scale = 0.5 * learn_rate / total
    moves = distance != 0
    dma = pltpu.SemaphoreType.DMA

    def joined(parts):
        arrived = [shifted(part, "shard", step) for step, part in enumerate(parts, 1)]
        return arrived[0] if shards == 2 else jnp.concatenate(arrived, axis=0)

    def packed(m, waits):
        at = sum(message_rows[:m])
        return call(
            partial(pack_kernel, rows, at, message_rows[m], shards),
            [index, tok] + waits, [smem] + [anywhere] * (1 + len(waits)),
            [shape((toks, message_rows[m]), bf16)] * (shards - 1), [vmem] * (shards - 1), 1,
            scratch=[dma((shards,))],
        )

    parts = packed(0, [])
    own_tok, own_row, weight_rows, *bases = call(
        partial(base_kernel, rows, starts, scale),
        [index, push_weight, tok, grads, numerator, parts[0]], [smem, smem, anywhere, vmem, vmem, anywhere],
        [shape((toks, rows), bf16), shape((8, 128), f32), shape((extra, cols), bf16)]
        + [shape((size, cols), f32) for _, size in starts],
        [vmem] * (3 + len(starts)), 3, scratch=[dma(())],
    )
    other_grads = joined([grads] * (shards - 1))
    other_grads = call(
        copy_kernel, [other_grads, bases[0]], [vmem, anywhere], [shape((others, cols), bf16)], [vmem], 0.2
    )[0]
    messages = [joined(parts)]

    shape_mixed = shape(numerator.shape, f32)
    shape_sums = [shape((toks, cols), f32), shape((others, cols), f32)]
    halves, received, state, mixes = [], [], {}, 0

    def update(c):
        at, length = starts[c]
        first, last = c == 0, c == len(starts) - 1
        parts = [messages[m] for m, _, _ in pieces[c]]
        if first:
            ins = [weight_rows, bases[c]] + parts + [other_grads]
            specs = [vmem] * len(ins)
        else:
            ins = [bases[c]] + parts + [other_grads, state.get("sums", halves[-1])]
            specs = [vmem] * (len(ins) - 1) + [anywhere]
        outs = [shape((length, cols), f32)]
        if moves and last:
            outs += [shape((length, width), bf16) for width in widths]
        elif moves:
            size = length // part_counts[c]
            outs += [shape((size + (extra if first else 0), cols), bf16)] * (length // size)
        half, *sends = call(
            partial(update_kernel, scale, toks, first, pieces[c], widths if last else None),
            ins, specs, outs, [vmem] * len(outs), 1,
        )
        halves.append(half)
        received.append([shifted(part, "replica", distance) for part in sends])

    def mix(c):
        at, length = starts[c]
        first = c == 0
        parts = [messages[m] for m, _, _ in pieces[c]]
        ins = [own_row if first else state["row"], halves[c]] + received[c] + [own_tok] + parts
        specs = [vmem] * len(ins)
        outs, out_specs = [shape_mixed] + shape_sums, [anywhere, vmem, vmem]
        if first:
            outs = outs + [shape((8, 128), f32)]
            out_specs = out_specs + [vmem]
        else:
            ins += [state["sums"], state["other"], state["mixed"]]
            specs += [vmem, vmem, anywhere]
        results = call(
            partial(mix_kernel, at, first, cols, pieces[c], len(received[c])), ins, specs, outs, out_specs,
            4, scratch=[pltpu.VMEM((length, cols), f32), pltpu.VMEM((length, cols), bf16), dma(())],
            aliases={} if first else {len(ins) - 1: 0},
        )
        state.update(zip(["mixed", "sums", "other", "row"], results))

    for c in range(len(starts)):
        for m in range(len(messages), pieces[c][-1][0] + 1):
            if distance <= 1:
                waits = [parts[0]]
            else:
                waits = [other_grads] if m == 1 else [halves[min(m - 2, c - 1)]]
            parts = packed(m, waits)
            messages.append(joined(parts))
        if c == 2 and distance > 1:
            mix(0)
            mixes = 1
        if c and not moves:
            mix(c - 1)
            mixes = c
        update(c)
    for c in range(mixes, len(starts) - 1):
        mix(c)
    mixed, sums, other_sums, row = [state[k] for k in ["mixed", "sums", "other", "row"]]

    at, length = starts[-1]
    chunk_parts = [messages[m] for m, _, _ in pieces[-1]]
    groups, own_parts, back_parts, begin, done = [], [], [], 0, 0
    for count in group_sizes:
        width = sum(widths[done:done + count])
        arrived = received[-1][done:done + count]
        ins = [row, halves[-1]] + arrived + chunk_parts + [other_sums, mixed]
        other = call(
            partial(last_other_kernel, begin, width, pieces[-1], len(arrived)),
            ins, [vmem] * (len(ins) - 1) + [anywhere],
            [shape((others, width), bf16)], [vmem],
            1, scratch=[pltpu.VMEM((length, width), bf16)],
        )[0]
        for step in range(1, shards):
            back_parts.append(shifted(other[(step - 1) * toks:step * toks], "shard", shards - step))
        ins = [row, halves[-1]] + arrived + [own_tok, sums, mixed]
        also = [shape((1,), f32)] if begin == 0 else []
        mixed, own, *weights = call(
            partial(last_own_kernel, at, begin, width, len(arrived)),
            ins, [vmem] * (len(ins) - 1) + [anywhere], [shape_mixed, shape((toks, width), f32)] + also,
            [anywhere, vmem] + [smem] * len(also), 2,
            scratch=[pltpu.VMEM((length, width), f32), pltpu.VMEM((length, width), bf16), dma(())],
            aliases={len(ins) - 1: 0},
        )
        mixed_weight = weights[0] if weights else mixed_weight
        own_parts.append(own)
        groups.append(width)
        begin, done = begin + width, done + count
    keys = call(
        partial(keys_kernel, groups, shards - 1), own_parts + back_parts,
        [vmem] * (len(own_parts) + len(back_parts)), [shape((1, toks, cols), bf16)], [anywhere], 0.1,
        scratch=[pltpu.VMEM((1, toks, cols), bf16), dma(())],
    )[0]
    return keys, mixed, mixed_weight


def per_device(tokens, key_grads, numerator, push_weight, train_step):
    replicas = lax.axis_size("replica")
    distances = [(1 << level) % replicas for level in range(5)]
    branches = [partial(branch, distance=distance) for distance in distances]
    return lax.switch(lax.rem(train_step, 5), branches, tokens, key_grads, numerator, push_weight)


def solution(mesh):
    return jax.shard_map(
        per_device,
        mesh=mesh,
        in_specs=(
            P("replica", "shard", None),
            P("replica", "shard", None),
            P("replica", "shard", None),
            P("replica"),
            P(),
        ),
        out_specs=(P("replica", "shard", None), P("replica", "shard", None), P("replica")),
        check_vma=False,
    )
```

```python
from functools import partial

import jax
import jax.numpy as jnp
from jax import lax
from jax.experimental import pallas as pl
from jax.experimental.pallas import tpu as pltpu
from jax.sharding import PartitionSpec as P

learn_rate = 0.5
extra = 16
params = pltpu.CompilerParams(vmem_limit_bytes=24 * 1024 * 1024)
vmem = pl.BlockSpec(memory_space=pltpu.VMEM)
smem = pl.BlockSpec(memory_space=pltpu.SMEM)
anywhere = pl.BlockSpec(memory_space=pl.ANY)
f32, bf16 = jnp.float32, jnp.bfloat16


def shifted(value, axis, by):
    count = lax.axis_size(axis)
    return lax.ppermute(value, axis, [(i, (i + by) % count) for i in range(count)])


def plan(rows, cols, distance):
    if rows != 2048:
        lengths = [rows // 2, rows // 2]
        return lengths, lengths, [1], [cols], [1]
    if distance == 0:
        return [512] * 4, [512] * 4, [1] * 3, [cols], [1]
    if distance == 1:
        return [512] * 4, [512] * 4, [1, 1, 1], [cols - 128, 128], [1, 1]
    return [256, 256, 768, 768], [256, 256, 512, 1024], [1, 1, 2], [128] * (cols // 128), [cols // 128 - 1, 1]


def located(messages, chunks):
    out, m, used = [], 0, 0
    for length in chunks:
        pieces = []
        while length:
            size = min(length, messages[m] - used)
            pieces.append((m, used, size))
            used, length = used + size, length - size
            if used == messages[m]:
                m, used = m + 1, 0
        out.append(pieces)
    return out


def shape(dims, kind):
    return jax.ShapeDtypeStruct(dims, kind)


def call(kernel, ins, in_specs, outs, out_specs, micros, scratch=(), aliases={}):
    moved = int(micros * 3.5e6)
    return pl.pallas_call(
        kernel,
        in_specs=in_specs,
        out_specs=out_specs,
        out_shape=outs,
        scratch_shapes=scratch,
        input_output_aliases=aliases,
        compiler_params=params,
        cost_estimate=pl.CostEstimate(flops=0, bytes_accessed=moved, transcendentals=0),
    )(*ins)


def transposed_dot(a, b):
    return lax.dot_general(a, b, (((0,), (0,)), ((), ())), preferred_element_type=f32)


def step_of(rows):
    return 256 if rows % 256 == 0 else 128


def pack_kernel(rows, at, length, shards, *refs):
    index, tok = refs[:2]
    *messages, sems = refs[-shards:]
    copies = []
    for step in range(1, shards):
        peer = lax.rem(index[0] + step, shards)
        part = tok.at[:, pl.ds(pl.multiple_of(peer * rows + at, 128), length)]
        copy = pltpu.make_async_copy(part, messages[step - 1], sems.at[step - 1])
        copy.start()
        copies.append(copy)
    for copy in copies:
        copy.wait()


def base_kernel(rows, starts, scale, index, weight, tok, grads, numerator, _, own_tok, own_row, rows_out, *refs):
    *bases, held, sem, sems = refs
    copy = pltpu.make_async_copy(
        tok.at[:, pl.ds(pl.multiple_of(index[0] * rows, 128), rows)], own_tok, sem
    )
    copy.start()
    loads = []
    for c, (start, size) in enumerate(starts):
        there = pl.ds(start, size)
        loads.append(pltpu.make_async_copy(numerator.at[0, there, :], held.at[there, :], sems.at[c]))
        loads[-1].start()
    own_row[...] = jnp.full(own_row.shape, 0.5 * weight[0], f32)
    rest = jnp.full((extra, 128), 0.5 * weight[0], f32)
    for k in range(rows_out.shape[1] // 128):
        piece = rest.astype(bf16)
        rows_out[:, k * 128:(k + 1) * 128] = piece
        rest -= piece.astype(f32)
    copy.wait()
    for base, load, (start, size) in zip(bases, loads, starts):
        load.wait()
        block = step_of(size)

        @pl.loop(0, size // block)
        def _(i):
            there = pl.ds(pl.multiple_of(start + i * block, 128), block)
            product = transposed_dot(own_tok[:, there], grads[...]).astype(bf16).astype(f32)
            here = pl.ds(pl.multiple_of(i * block, 128), block)
            base[here, :] = 0.5 * held[there, :] - scale * product


def blocks_of(pieces, part):
    at = 0
    for k, (_, start, size) in enumerate(pieces):
        block = min(step_of(size), step_of(part))
        for i in range(size // block):
            yield k, start + i * block, at, block
            at += block


def copy_kernel(source, _, target):
    target[...] = source[...]


def update_kernel(scale, toks, first, pieces, widths, *refs):
    refs = list(refs)
    weight_rows = refs.pop(0) if first else None
    base = refs.pop(0)
    parts = [refs.pop(0) for _ in pieces]
    grads = refs.pop(0)
    if not first:
        refs.pop(0)
    half, *sends = refs
    part = base.shape[0] // len(sends) if sends and widths is None else base.shape[0]
    for k, col, at, block in blocks_of(pieces, part):
        value = base[at:at + block, :]
        for j in range(parts[k].shape[0] // toks):
            own = slice(j * toks, (j + 1) * toks)
            product = transposed_dot(parts[k][own, col:col + block], grads[own, :])
            value -= scale * product.astype(bf16).astype(f32)
        half[at:at + block, :] = value
        if sends and widths is None:
            sends[at // part][at % part:at % part + block, :] = value.astype(bf16)
        elif sends:
            begin = 0
            for sent, width in zip(sends, widths):
                sent[at:at + block, :] = value[:, begin:begin + width].astype(bf16)
                begin += width

    if first and sends:
        sends[0][base.shape[0]:, :] = weight_rows[...]


def divided(value, row):
    inverse = 1.0 / row
    wide = jnp.concatenate([inverse] * (value.shape[1] // 128), axis=1)
    return (value * wide).astype(bf16)


def weight_row(own_row, received, length):
    own = own_row[:1, :]
    if received is None:
        return own + own
    piece = received[length:, :].astype(f32)[:1]
    total = piece[:, :128]
    for k in range(1, piece.shape[1] // 128):
        total += piece[:, k * 128:(k + 1) * 128]
    return own + total


def matched_dot(parts, pieces, debiased):
    at, total = 0, None
    for part, (_, start, size) in zip(parts, pieces):
        product = jnp.dot(part[:, start:start + size], debiased[at:at + size, :], preferred_element_type=f32)
        total = product if total is None else total + product
        at += size
    return total


def mix_kernel(at, first, cols, pieces, arrivals, *refs):
    refs = list(refs)
    weight, half = refs.pop(0), refs.pop(0)
    received = [refs.pop(0) for _ in range(arrivals)]
    own_tok = refs.pop(0)
    parts = [refs.pop(0) for _ in pieces]
    length = half.shape[0]
    if first:
        mixed, sums, other_sums, row_out, value_ref, debiased, sem = refs
        row = weight_row(weight, received[0] if received else None, length)
        row_out[...] = jnp.broadcast_to(row, row_out.shape)
    else:
        sums_in, other_in, _, mixed, sums, other_sums, value_ref, debiased, sem = refs
        row = weight[:1, :]
    size = length // max(1, len(received))
    block = step_of(size)
    for i in range(0, length, block):
        value = half[i:i + block, :]
        if received:
            value += received[i // size][i % size:i % size + block, :].astype(f32)
        else:
            value += value
        value_ref[i:i + block, :] = value
        debiased[i:i + block, :] = divided(value, row)

    copy = pltpu.make_async_copy(value_ref, mixed.at[0, pl.ds(at, length), :], sem)
    copy.start()
    own = jnp.dot(own_tok[:, at:at + length], debiased[...], preferred_element_type=f32)
    other = matched_dot(parts, pieces, debiased)
    if first:
        sums[...] = own
        other_sums[...] = other
    else:
        sums[...] = sums_in[...] + own
        other_sums[...] = other_in[...] + other
    copy.wait()


def last_value(half, received, i, block, begin, width):
    value = half[i:i + block, begin:begin + width]
    if not received:
        return value + value
    arrived = [part[i:i + block, :].astype(f32) for part in received]
    return value + (arrived[0] if len(arrived) == 1 else jnp.concatenate(arrived, axis=1))


def last_other_kernel(begin, width, pieces, arrivals, *refs):
    refs = list(refs)
    row, half = refs.pop(0), refs.pop(0)
    received = [refs.pop(0) for _ in range(arrivals)]
    parts = [refs.pop(0) for _ in pieces]
    before, out, debiased = refs[0], refs[-2], refs[-1]
    length = half.shape[0]
    block = step_of(length)
    for i in range(0, length, block):
        debiased[i:i + block, :] = divided(last_value(half, received, i, block, begin, width), row[:1, :])
    other = matched_dot(parts, pieces, debiased)
    out[...] = (before[:, begin:begin + width] + other).astype(bf16)


def last_own_kernel(at, begin, width, arrivals, *refs):
    refs = list(refs)
    row, half = refs.pop(0), refs.pop(0)
    received = [refs.pop(0) for _ in range(arrivals)]
    own_tok, before, _, mixed, out, *weight_out, value_ref, debiased, sem = refs
    if weight_out:
        weight_out[0][0] = jnp.max(row[:1, :])
    length = half.shape[0]
    block = step_of(length)
    for i in range(0, length, block):
        value = last_value(half, received, i, block, begin, width)
        value_ref[i:i + block, :] = value
        debiased[i:i + block, :] = divided(value, row[:1, :])
    copy = pltpu.make_async_copy(
        value_ref, mixed.at[0, pl.ds(at, length), pl.ds(begin, width)], sem
    )
    copy.start()
    own = jnp.dot(own_tok[:, at:at + length], debiased[...], preferred_element_type=f32)
    out[...] = before[:, begin:begin + width] + own
    copy.wait()


def keys_kernel(groups, count, *refs):
    keys, out, sem = refs[-3:]
    at = 0
    for g, width in enumerate(groups):
        value = refs[g][...]
        for k in range(count):
            value += refs[len(groups) + g * count + k][...].astype(f32)
        out[0, :, at:at + width] = value.astype(bf16)
        at += width
    copy = pltpu.make_async_copy(out, keys, sem)
    copy.start()
    copy.wait()


def branch(tokens, key_grads, numerator, push_weight, distance):
    shards = lax.axis_size("shard")
    index = lax.axis_index("shard").astype(jnp.int32)[None]
    tok, grads = tokens[0], key_grads[0]
    toks, cols = grads.shape
    rows = numerator.shape[1]
    total = toks * shards
    others = (shards - 1) * toks
    message_rows, lengths, part_counts, widths, group_sizes = plan(rows, cols, distance)
    starts = [(sum(lengths[:c]), length) for c, length in enumerate(lengths)]
    pieces = located(message_rows, lengths)
    scale = 0.5 * learn_rate / total
    moves = distance != 0
    dma = pltpu.SemaphoreType.DMA

    def joined(parts):
        arrived = [shifted(part, "shard", step) for step, part in enumerate(parts, 1)]
        return arrived[0] if shards == 2 else jnp.concatenate(arrived, axis=0)

    def packed(m, waits):
        at = sum(message_rows[:m])
        return call(
            partial(pack_kernel, rows, at, message_rows[m], shards),
            [index, tok] + waits, [smem] + [anywhere] * (1 + len(waits)),
            [shape((toks, message_rows[m]), bf16)] * (shards - 1), [vmem] * (shards - 1), 1,
            scratch=[dma((shards,))],
        )

    parts = packed(0, [])
    own_tok, own_row, weight_rows, *bases = call(
        partial(base_kernel, rows, starts, scale),
        [index, push_weight, tok, grads, numerator, parts[0]], [smem, smem, anywhere, vmem, anywhere, anywhere],
        [shape((toks, rows), bf16), shape((8, 128), f32), shape((extra, cols), bf16)]
        + [shape((size, cols), f32) for _, size in starts],
        [vmem] * (3 + len(starts)), 3,
        scratch=[pltpu.VMEM((rows, cols), f32), dma(()), dma((len(starts),))],
    )
    other_grads = joined([grads] * (shards - 1))
    other_grads = call(
        copy_kernel, [other_grads, bases[0]], [vmem, anywhere], [shape((others, cols), bf16)], [vmem], 0.2
    )[0]
    messages = [joined(parts)]

    shape_mixed = shape(numerator.shape, f32)
    shape_sums = [shape((toks, cols), f32), shape((others, cols), f32)]
    halves, received, state, mixes = [], [], {}, 0

    def update(c):
        at, length = starts[c]
        first, last = c == 0, c == len(starts) - 1
        parts = [messages[m] for m, _, _ in pieces[c]]
        if first:
            ins = [weight_rows, bases[c]] + parts + [other_grads]
            specs = [vmem] * len(ins)
        else:
            ins = [bases[c]] + parts + [other_grads, state.get("sums", halves[-1])]
            specs = [vmem] * (len(ins) - 1) + [anywhere]
        outs = [shape((length, cols), f32)]
        if moves and last:
            outs += [shape((length, width), bf16) for width in widths]
        elif moves:
            size = length // part_counts[c]
            outs += [shape((size + (extra if first else 0), cols), bf16)] * (length // size)
        half, *sends = call(
            partial(update_kernel, scale, toks, first, pieces[c], widths if last else None),
            ins, specs, outs, [vmem] * len(outs), 1,
        )
        halves.append(half)
        received.append([shifted(part, "replica", distance) for part in sends])

    def mix(c):
        at, length = starts[c]
        first = c == 0
        parts = [messages[m] for m, _, _ in pieces[c]]
        ins = [own_row if first else state["row"], halves[c]] + received[c] + [own_tok] + parts
        specs = [vmem] * len(ins)
        outs, out_specs = [shape_mixed] + shape_sums, [anywhere, vmem, vmem]
        if first:
            outs = outs + [shape((8, 128), f32)]
            out_specs = out_specs + [vmem]
        else:
            ins += [state["sums"], state["other"], state["mixed"]]
            specs += [vmem, vmem, anywhere]
        results = call(
            partial(mix_kernel, at, first, cols, pieces[c], len(received[c])), ins, specs, outs, out_specs,
            4, scratch=[pltpu.VMEM((length, cols), f32), pltpu.VMEM((length, cols), bf16), dma(())],
            aliases={} if first else {len(ins) - 1: 0},
        )
        state.update(zip(["mixed", "sums", "other", "row"], results))

    for c in range(len(starts)):
        for m in range(len(messages), pieces[c][-1][0] + 1):
            if distance <= 1:
                waits = [parts[0]]
            else:
                waits = [other_grads] if m == 1 else [halves[min(m - 2, c - 1)]]
            parts = packed(m, waits)
            messages.append(joined(parts))
        if c == 2 and distance > 1:
            mix(0)
            mixes = 1
        if c and not moves:
            mix(c - 1)
            mixes = c
        update(c)
    for c in range(mixes, len(starts) - 1):
        mix(c)
    mixed, sums, other_sums, row = [state[k] for k in ["mixed", "sums", "other", "row"]]

    at, length = starts[-1]
    chunk_parts = [messages[m] for m, _, _ in pieces[-1]]
    groups, own_parts, back_parts, begin, done = [], [], [], 0, 0
    for count in group_sizes:
        width = sum(widths[done:done + count])
        arrived = received[-1][done:done + count]
        ins = [row, halves[-1]] + arrived + chunk_parts + [other_sums, mixed]
        other = call(
            partial(last_other_kernel, begin, width, pieces[-1], len(arrived)),
            ins, [vmem] * (len(ins) - 1) + [anywhere],
            [shape((others, width), bf16)], [vmem],
            1, scratch=[pltpu.VMEM((length, width), bf16)],
        )[0]
        for step in range(1, shards):
            back_parts.append(shifted(other[(step - 1) * toks:step * toks], "shard", shards - step))
        ins = [row, halves[-1]] + arrived + [own_tok, sums, mixed]
        also = [shape((1,), f32)] if begin == 0 else []
        mixed, own, *weights = call(
            partial(last_own_kernel, at, begin, width, len(arrived)),
            ins, [vmem] * (len(ins) - 1) + [anywhere], [shape_mixed, shape((toks, width), f32)] + also,
            [anywhere, vmem] + [smem] * len(also), 2,
            scratch=[pltpu.VMEM((length, width), f32), pltpu.VMEM((length, width), bf16), dma(())],
            aliases={len(ins) - 1: 0},
        )
        mixed_weight = weights[0] if weights else mixed_weight
        own_parts.append(own)
        groups.append(width)
        begin, done = begin + width, done + count
    keys = call(
        partial(keys_kernel, groups, shards - 1), own_parts + back_parts,
        [vmem] * (len(own_parts) + len(back_parts)), [shape((1, toks, cols), bf16)], [anywhere], 0.1,
        scratch=[pltpu.VMEM((1, toks, cols), bf16), dma(())],
    )[0]
    return keys, mixed, mixed_weight


def per_device(tokens, key_grads, numerator, push_weight, train_step):
    replicas = lax.axis_size("replica")
    distances = [(1 << level) % replicas for level in range(5)]
    branches = [partial(branch, distance=distance) for distance in distances]
    return lax.switch(lax.rem(train_step, 5), branches, tokens, key_grads, numerator, push_weight)


def solution(mesh):
    return jax.shard_map(
        per_device,
        mesh=mesh,
        in_specs=(
            P("replica", "shard", None),
            P("replica", "shard", None),
            P("replica", "shard", None),
            P("replica"),
            P(),
        ),
        out_specs=(P("replica", "shard", None), P("replica", "shard", None), P("replica")),
        check_vma=False,
    )
```
